256 devices in a mesh: tok: 4 (over x), vocab: 64 (over y, z, core).
Axes of the slice: x: 4, y: 4, z: 8, core: 2. Of those that a mesh axis runs over, the one named last changes fastest.
Arguments:
- hidden: bfloat16 [512, 4608], P('tok', 'vocab'), may hold values from -6 to 6
- weight: bfloat16 [131072, 4608], P(('tok', 'vocab')), may hold values from -0.75 to 0.75
- targets: int32 [512], P('tok'), may hold values from 0 to 131071
Outputs:
- loss: float32 [512], P('tok')
- grad_hidden: bfloat16 [512, 4608], P('tok', 'vocab')
- grad_weight: bfloat16 [131072, 4608], P(('tok', 'vocab'))
The draws below stay inside these ranges and needn't reach their ends.
All inputs are finite; a program needn't handle non-finite values.
Results may differ from the reference program's by a relative error of at most 0.0038.
Values may be sent and summed in bfloat16 or wider, within the bound.
No kernel may reach another device: no remote copies, remote signals or barrier semaphores. Data moves between devices by JAX's collectives and lax.ppermute only.
A program may use at most 64 MiB of HBM per device.

```python
import jax
import jax.numpy as jnp
from jax import lax

D = 4608
V = 131072
CAP = 30
TOKENS = 512


def place_ends(array, own_key, smallest, high):
    extent = array.shape
    spot = [jax.random.randint(jax.random.fold_in(own_key, axis), (), 0, extent[axis]) for axis in range(len(extent))]
    array = array.at[tuple(spot)].set(smallest)
    longest = extent.index(max(extent))
    spot[longest] = (spot[longest] + 1) % extent[longest]
    return array.at[tuple(spot)].set(high)


def block_levels(stream_key, shape, pieces, low, high):
    level, own = 1.0, jax.random.fold_in(stream_key, 6)
    for dim, shards_of in pieces:
        heights = jnp.exp(jax.random.uniform(jax.random.fold_in(own, dim), (shards_of,), jnp.float32, low / len(pieces), high / len(pieces)))
        level = level * jnp.repeat(heights, shape[dim] // shards_of).reshape([-1 if axis == dim else 1 for axis in range(len(shape))])
    return level


def gaussian(own_key, dims, width, reach, pieces=(), kind=jnp.bfloat16):
    loudness = block_levels(own_key, dims, pieces, -0.22, 0.18) if pieces else 1.0
    values = jax.random.normal(own_key, dims, jnp.float32) * width * loudness
    return jnp.minimum(jnp.maximum(values, -reach), reach).astype(kind)


def setup_inputs(seed: int = 0) -> dict:
    splits = jax.random.split(jax.random.key(seed), 4)
    return {
        "hidden": gaussian(splits[0], (TOKENS, D), 1.0, 6.0, ((0, 4), (1, 64))),
        "weight": gaussian(splits[1], (V, D), (D // 64) ** -0.5, 0.75, ((0, 256),)),
        "targets": place_ends(jax.random.randint(splits[2], (TOKENS,), 0, V), jax.random.fold_in(splits[2], 1), 0, V - 1).astype(jnp.int32),
    }


def reference(hidden, weight, targets):
    block = min(8192, V)
    count = V // block
    blocks = weight.reshape(count, block, D)
    starts = jnp.arange(count, dtype=jnp.int32) * block

    def capped_of(wblock):
        logits = lax.dot_general(hidden, wblock, (((1,), (1,)), ((), ())), preferred_element_type=jnp.float32)
        return CAP * jnp.tanh(logits / CAP)

    def first_pass(carry, item):
        wblock, start = item
        capped = capped_of(wblock)
        columns = start + jnp.arange(block, dtype=jnp.int32)
        hit = columns[None, :] == targets[:, None]
        total = carry[0] + jnp.sum(jnp.exp(capped - CAP), axis=1)
        picked = carry[1] + jnp.sum(jnp.where(hit, capped, 0.0), axis=1)
        return (total, picked), None

    zeros = jnp.zeros((TOKENS,), jnp.float32)
    (total, picked), _ = lax.scan(first_pass, (zeros, zeros), (blocks, starts))
    lse = CAP + jnp.log(total)
    loss = lse - picked

    def second_pass(carry, item):
        wblock, start = item
        capped = capped_of(wblock)
        columns = start + jnp.arange(block, dtype=jnp.int32)
        hit = (columns[None, :] == targets[:, None]).astype(jnp.float32)
        probs = jnp.exp(capped - lse[:, None])
        dlogits = ((probs - hit) * (1.0 - (capped / CAP) ** 2)).astype(jnp.bfloat16)
        carry = carry + jnp.dot(dlogits, wblock, preferred_element_type=jnp.float32)
        gw = lax.dot_general(dlogits, hidden, (((0,), (0,)), ((), ())), preferred_element_type=jnp.float32)
        return carry, gw.astype(jnp.bfloat16)

    gh, gw_blocks = lax.scan(second_pass, jnp.zeros((TOKENS, D), jnp.float32), (blocks, starts))
    return loss, gh.astype(jnp.bfloat16), gw_blocks.reshape(V, D)
```

```python
import jax
import jax.numpy as jnp
from jax import lax
from jax.sharding import Mesh, PartitionSpec as P

CAP = 30
F32, BF16 = jnp.float32, jnp.bfloat16
X, Y, Z, C = 4, 4, 8, 2


def pull(array, axis, size, step):
    return lax.ppermute(array, axis, [((i + step) % size, i) for i in range(size)])


def push(array, axis, size, step):
    return lax.ppermute(array, axis, [(i, (i + step) % size) for i in range(size)])


def turned(array, start, size, dim):
    doubled = lax.concatenate([array, array], dim)
    return lax.dynamic_slice_in_dim(doubled, start, size, dim)


def spread(array, axes, size):
    copies = jnp.broadcast_to(array[None], (size,) + array.shape)
    return lax.all_to_all(copies, axes, 0, 0, tiled=True)


def digits(targets):
    parts = [targets // 65536, (targets // 256) % 256, targets % 256]
    return jnp.concatenate([jnp.stack(parts), jnp.zeros((5, targets.shape[0]), jnp.int32)]).astype(BF16)


def undigits(rows):
    parts = rows.astype(jnp.int32)
    return parts[:, 0] * 65536 + parts[:, 1] * 256 + parts[:, 2]


def per_device(hidden, weight, targets):
    rows, feats = hidden.shape
    voc = weight.shape[0]
    half = Z // 2
    x, y, z, c = (lax.axis_index(name) for name in ("x", "y", "z", "c"))

    wt = weight.T.reshape(Y, Z, C, feats, voc)
    wt = turned(wt, y, Y, 0)
    mine = lax.dynamic_index_in_dim(wt, c, 2, keepdims=False)
    theirs = lax.dynamic_index_in_dim(wt, 1 - c, 2, keepdims=False)
    pair = jnp.concatenate([mine, pull(theirs, "c", C, 1)], -1)

    along_z = spread(hidden.T, "z", Z)
    a, b = along_z[:half], along_z[half:]
    b = jnp.concatenate([b.reshape(half * feats, rows), digits(targets)])
    a_y, b_x = [a], [b]
    for step in range(1, 4):
        a_y.append(pull(a, "y", Y, step))
        b_x.append(pull(b, "x", X, step))
    a2 = jnp.stack(a_y)
    b2 = jnp.stack(b_x)
    tgt = undigits(b2[:, half * feats :]).reshape(X * rows)
    b2 = b2[:, : half * feats]
    a_xy, b_xy = [a2], [b2]
    for step in range(1, 4):
        a_xy.append(pull(a2, "x", X, step))
        b_xy.append(pull(b2, "y", Y, step))
    a3 = jnp.stack(a_xy, 3).reshape(Y, half, feats, X * rows)
    b3 = jnp.stack(b_xy).reshape(Y, X, half, feats, rows)
    b3 = b3.transpose(0, 2, 3, 1, 4).reshape(Y, half, feats, X * rows)
    ht = jnp.concatenate([a3, b3], 1)

    part = lax.dot_general(
        pair.reshape(-1, C * voc), ht.reshape(-1, X * rows), (((0,), (0,)), ((), ())), preferred_element_type=F32
    )
    logits = part[:voc] + pull(part[voc:], "c", C, 1)
    capped = CAP * jnp.tanh(logits / CAP)
    offset = (((x * Y + y) * Z + z) * C + c) * voc
    columns = offset + jnp.arange(voc, dtype=jnp.int32)
    hit = columns[:, None] == tgt[None, :]
    stats = jnp.stack([jnp.sum(jnp.exp(capped - CAP), 0), jnp.sum(jnp.where(hit, capped, 0.0), 0)])
    stats = spread(stats.reshape(2, X, rows), ("z", "c"), Z * C).sum(0)
    stats = turned(stats, (X - x) % X, X, 1)
    stats = spread(stats, ("x", "y"), X * Y).sum(0)
    stats = turned(stats, x, X, 1)
    lse = CAP + jnp.log(stats[0])
    loss = lse[0] - stats[1, 0]
    probs = jnp.exp(capped - lse.reshape(1, X * rows))
    dlogits = ((probs - hit.astype(F32)) * (1.0 - (capped / CAP) ** 2)).astype(BF16)

    dl_pair = jnp.concatenate([dlogits, pull(dlogits, "c", C, 1)], 0)
    grad = jnp.dot(pair.reshape(-1, C * voc), dl_pair, preferred_element_type=F32)
    grad = grad.reshape(Y, Z, feats, X, rows)
    ga, gb = grad[:, :half], grad[:, half:]
    a_own, b_own = ga[:, :, :, 0], gb[0]
    for step in range(1, 4):
        a_own = a_own + push(ga[:, :, :, step].astype(BF16), "x", X, step).astype(F32)
        b_own = b_own + push(gb[step].astype(BF16), "y", Y, step).astype(F32)
    a_sum, b_sum = a_own[0], b_own[:, :, 0]
    for step in range(1, 4):
        a_sum = a_sum + push(a_own[step].astype(BF16), "y", Y, step).astype(F32)
        b_sum = b_sum + push(b_own[:, :, step].astype(BF16), "x", X, step).astype(F32)
    by_z = lax.all_to_all(jnp.concatenate([a_sum, b_sum], 0), "z", 0, 0, tiled=True)
    grad_hidden = by_z.sum(0).astype(BF16).T

    other = pull(ht, "c", C, 1)
    first = jnp.where(c == 0, ht, other)
    second = jnp.where(c == 0, other, ht)
    full = turned(jnp.stack([first, second], 2), (Y - y) % Y, Y, 0)
    full = full.reshape(Y * Z * C * feats, X * rows)
    grad_weight = lax.dot_general(
        dlogits, full, (((1,), (1,)), ((), ())), preferred_element_type=F32
    ).astype(BF16)
    return loss, grad_hidden, grad_weight


def solution(mesh):
    chips = Mesh(mesh.devices.reshape(X, Y, Z, C), ("x", "y", "z", "c"))
    in_specs = (P("x", ("y", "z", "c")), P(("x", "y", "z", "c"), None), P("x"))
    out_specs = (P("x"), P("x", ("y", "z", "c")), P(("x", "y", "z", "c"), None))
    return jax.shard_map(per_device, mesh=chips, in_specs=in_specs, out_specs=out_specs, check_vma=False)
```

```python
import jax
import jax.numpy as jnp
from jax import lax
from jax.experimental import pallas as pl
from jax.experimental.pallas import tpu as pltpu
from jax.sharding import Mesh, PartitionSpec as P

CAP = 30
F32, BF16 = jnp.float32, jnp.bfloat16
X, Y, Z, C = 4, 4, 8, 2


def flip(array, axis, size, change):
    return lax.ppermute(array, axis, [(i, i ^ change) for i in range(size)])


def reordered(array, own, dim):
    return jnp.concatenate([lax.dynamic_slice_in_dim(array, own ^ k, 1, dim) for k in range(4)], dim)


def at_once(*arrays):
    return lax.optimization_barrier(arrays)


def spread(array, axes, size):
    copies = jnp.broadcast_to(array[None], (size,) + array.shape)
    return lax.all_to_all(copies, axes, 0, 0, tiled=True)


def digits(targets):
    parts = [targets // 65536, (targets // 256) % 256, targets % 256]
    return jnp.concatenate([jnp.stack(parts), jnp.zeros((5, targets.shape[0]), jnp.int32)]).astype(BF16)


def undigits(rows):
    parts = rows.astype(jnp.int32)
    return parts[:, 0] * 65536 + parts[:, 1] * 256 + parts[:, 2]


VMEM_LIMIT = 18 * 1024 * 1024


def fetch_columns(meta_ref, sources, slots, sems, wide):
    copies = []
    for step in range(Y):
        columns = pl.ds(pl.multiple_of(meta_ref[step], 128), wide)
        row = []
        for place, ref in enumerate(sources):
            row.append(pltpu.make_async_copy(ref.at[:, columns], slots.at[step, place], sems.at[step, place]))
        copies.append(row)
    for row in copies:
        for copy in row:
            copy.start()
    return copies


def in_hbm(arrays):
    return [pltpu.with_memory_space_constraint(array, pltpu.HBM) for array in arrays]


def logits_kernel(meta_ref, own_ref, other_ref, *refs):
    a_refs, b_refs = refs[:5], refs[5:10]
    mine_ref, theirs_ref, ht_ref, slots, tall, sems, piece_sems, out_sem = refs[10:]
    part, rows = a_refs[0].shape[1:]
    wide = slots.shape[-1]
    shift = pl.multiple_of(meta_ref[Y], 64)
    pieces = ((0, 0, Y), (1, 0, Y), (3, 0, Y), (2, 0, Y // 2), (2, Y // 2, Y // 2))
    a_copies, b_copies = [], [[] for _ in range(Y)]
    for i, (place, first, count) in enumerate(pieces):
        target = tall.at[pl.ds(first, count), pl.ds(shift, part), pl.ds(place * rows, rows)]
        a_copies.append(pltpu.make_async_copy(a_refs[i], target, piece_sems.at[Y, i]))
        for k in range(count):
            target = tall.at[place, pl.ds(shift + part, part), pl.ds((first + k) * rows, rows)]
            b_copies[place].append(pltpu.make_async_copy(b_refs[i].at[k], target, piece_sems.at[place, first + k]))
    for copy in a_copies:
        copy.start()
    for row in b_copies:
        for copy in row:
            copy.start()
    copies = fetch_columns(meta_ref, (own_ref, other_ref), slots, sems, wide)
    edge = wide - 2 * part
    zeros = jnp.zeros((edge, X * rows), tall.dtype)
    empty = pl.multiple_of(2 * part * (1 - meta_ref[Y] // edge), 64)
    for step in range(Y):
        tall[step, pl.ds(empty, edge)] = zeros
    for copy in a_copies:
        copy.wait()
    for step in range(Y):
        for copy in b_copies[step]:
            copy.wait()
        for place, out_ref in enumerate((mine_ref, theirs_ref)):
            copies[step][place].wait()
            term = jnp.dot(slots[step, place], tall[step], preferred_element_type=F32)
            if step == 0:
                out_ref[...] = term
            else:
                out_ref[...] += term
    keep = pltpu.make_async_copy(tall.at[:, pl.ds(shift, 2 * part)], ht_ref, out_sem)
    keep.start()
    keep.wait()


def logits_of(meta, own, other, a_pieces, b_pieces, wide):
    voc = own.shape[0]
    part, rows = a_pieces[0].shape[1:]
    vmem = pl.BlockSpec(memory_space=pltpu.VMEM)
    hbm = pl.BlockSpec(memory_space=pltpu.HBM)
    square = jax.ShapeDtypeStruct((voc, X * rows), F32)
    return pl.pallas_call(
        logits_kernel,
        out_shape=(square, square, pltpu.HBM((Y, 2 * part, X * rows), BF16)),
        in_specs=[pl.BlockSpec(memory_space=pltpu.SMEM), hbm, hbm] + [hbm] * 10,
        out_specs=(vmem, vmem, hbm),
        scratch_shapes=[
            pltpu.VMEM((Y, 2, voc, wide), BF16),
            pltpu.VMEM((Y, wide, X * rows), BF16),
            pltpu.SemaphoreType.DMA((Y, 2)),
            pltpu.SemaphoreType.DMA((Y + 1, 5)),
            pltpu.SemaphoreType.DMA,
        ],
        compiler_params=pltpu.CompilerParams(vmem_limit_bytes=VMEM_LIMIT),
        cost_estimate=pl.CostEstimate(
            flops=4 * Y * voc * wide * X * rows, bytes_accessed=4 * Y * voc * wide, transcendentals=0
        ),
    )(meta, *in_hbm([own, other, *a_pieces, *b_pieces]))


def turn_kernel(meta_ref, own_ref, other_ref, out_ref, slots, whole, made, sems, out_sems):
    part = out_ref.shape[2]
    voc, wide = slots.shape[2:]
    copies, outs = [], []
    for i in range(2 * Y):
        columns = pl.ds(pl.multiple_of(meta_ref[i], 128), wide)
        row = [
            pltpu.make_async_copy(ref.at[:, columns], slots.at[i, place], sems.at[i, place])
            for place, ref in enumerate((own_ref, other_ref))
        ]
        copies.append(row)
    for row in copies:
        for copy in row:
            copy.start()
    for i in range(2 * Y):
        shift = pl.multiple_of(meta_ref[2 * Y + i // Y], 32)
        for place in range(2):
            copies[i][place].wait()
            whole[i % 2, place] = slots[i, place].T
            made[i, :, place * voc : (place + 1) * voc] = whole[i % 2, place, pl.ds(shift, part)]
        out = pltpu.make_async_copy(made.at[i], out_ref.at[i % Y, i // Y], out_sems.at[i])
        out.start()
        outs.append(out)
    for out in outs:
        out.wait()


def turned_weights(meta, own, other, part, wide):
    voc = own.shape[0]
    hbm = pl.BlockSpec(memory_space=pltpu.HBM)
    return pl.pallas_call(
        turn_kernel,
        out_shape=pltpu.HBM((Y, 2, part, 2 * voc), BF16),
        in_specs=[pl.BlockSpec(memory_space=pltpu.SMEM), hbm, hbm],
        out_specs=hbm,
        scratch_shapes=[
            pltpu.VMEM((2 * Y, 2, voc, wide), BF16),
            pltpu.VMEM((2, 2, wide, voc), BF16),
            pltpu.VMEM((2 * Y, part, 2 * voc), BF16),
            pltpu.SemaphoreType.DMA((2 * Y, 2)),
            pltpu.SemaphoreType.DMA((2 * Y,)),
        ],
        compiler_params=pltpu.CompilerParams(vmem_limit_bytes=VMEM_LIMIT),
        cost_estimate=pl.CostEstimate(flops=0, bytes_accessed=12 * Y * voc * wide, transcendentals=0),
    )(meta, *in_hbm([own, other]))


def product(wt, dl, dlo):
    voc = dl.shape[0]
    return jnp.dot(wt[:, :voc], dl, preferred_element_type=F32) + jnp.dot(
        wt[:, voc:], dlo, preferred_element_type=F32
    )


FIRST_BLOCKS = ((0, 0), (1, 0), (2, 0), (3, 0), (2, 1))
REST_BLOCKS = ((0, 0), (1, 0), (2, 0), (3, 0), (0, 1), (1, 1), (3, 1))


def fetch_blocks(wt_ref, blocks, slots, sems):
    copies = []
    for i, (step, side) in enumerate(blocks):
        copies.append(pltpu.make_async_copy(wt_ref.at[step, side], slots.at[i], sems.at[i]))
    for copy in copies:
        copy.start()
    return copies


def first_kernel(wt_ref, dl_ref, dlo_ref, alo_ref, ahi_ref, blo_ref, bhi_ref, slots, sems):
    part, rows = alo_ref.shape[1:]
    copies = fetch_blocks(wt_ref, FIRST_BLOCKS, slots, sems)
    lanes = slice(2 * rows, 3 * rows)
    for i, (step, side) in enumerate(FIRST_BLOCKS):
        copies[i].wait()
        if side == 1:
            piece = product(slots[i], dl_ref[...], dlo_ref[...]).astype(BF16)
            blo_ref[...], bhi_ref[...] = piece[: part // 2], piece[part // 2 :]
            continue
        piece = product(slots[i], dl_ref[:, lanes], dlo_ref[:, lanes]).astype(BF16)
        if step < Y // 2:
            alo_ref[step] = piece
        else:
            ahi_ref[step - Y // 2] = piece


def rest_kernel(wt_ref, dl_ref, dlo_ref, *refs):
    a_outs, b_outs = refs[:3], refs[3:6]
    slots, sems = refs[6:]
    rows = a_outs[0].shape[2]
    copies = fetch_blocks(wt_ref, REST_BLOCKS, slots, sems)
    for i, (step, side) in enumerate(REST_BLOCKS):
        copies[i].wait()
        piece = product(slots[i], dl_ref[...], dlo_ref[...])
        if side == 1:
            b_outs[min(step, 2)][...] = piece
            continue
        for out_ref, place in zip(a_outs, (0, 1, 3)):
            out_ref[step] = piece[:, place * rows : (place + 1) * rows]


def gradient_call(kernel, blocks, outs, wt, dl, dlo):
    vmem = pl.BlockSpec(memory_space=pltpu.VMEM)
    part, wide = wt.shape[2:]
    count = len(blocks)
    return pl.pallas_call(
        kernel,
        out_shape=tuple(outs),
        in_specs=[pl.BlockSpec(memory_space=pltpu.HBM), vmem, vmem],
        out_specs=tuple([vmem] * len(outs)),
        scratch_shapes=[pltpu.VMEM((count, part, wide), BF16), pltpu.SemaphoreType.DMA((count,))],
        compiler_params=pltpu.CompilerParams(vmem_limit_bytes=VMEM_LIMIT),
        cost_estimate=pl.CostEstimate(
            flops=2 * count * part * wide * dl.shape[1], bytes_accessed=2 * count * part * wide, transcendentals=0
        ),
    )(*in_hbm([wt]), dl, dlo)


def weight_kernel(places_ref, dl_ref, here_ref, there_ref, out_ref, both):
    half = here_ref.shape[1]
    core = places_ref[Y]
    both[pl.ds(pl.multiple_of(core * half, 64), half)] = here_ref[0]
    both[pl.ds(pl.multiple_of((1 - core) * half, 64), half)] = there_ref[0]
    over_last = (((1,), (1,)), ((), ()))
    out_ref[...] = lax.dot_general(dl_ref[...], both[...], over_last, preferred_element_type=F32).astype(BF16)


def weight_of(places, dl, here, there):
    voc, all_rows = dl.shape
    half = here.shape[1]
    one = pl.BlockSpec((1, half, all_rows), lambda i, places: (i, 0, 0))
    return pl.pallas_call(
        weight_kernel,
        out_shape=jax.ShapeDtypeStruct((voc, Y * 2 * half), BF16),
        grid_spec=pltpu.PrefetchScalarGridSpec(
            num_scalar_prefetch=1,
            grid=(Y,),
            in_specs=[pl.BlockSpec((voc, all_rows), lambda i, places: (0, 0)), one, one],
            out_specs=pl.BlockSpec((voc, 2 * half), lambda i, places: (0, places[i])),
            scratch_shapes=[pltpu.VMEM((2 * half, all_rows), BF16)],
        ),
        compiler_params=pltpu.CompilerParams(vmem_limit_bytes=VMEM_LIMIT),
        cost_estimate=pl.CostEstimate(
            flops=4 * Y * voc * half * all_rows, bytes_accessed=8 * Y * half * all_rows, transcendentals=0
        ),
    )(places, dl, *in_hbm([here, there]))


def per_device(hidden, weight, targets):
    rows, feats = hidden.shape
    voc = weight.shape[0]
    block = Z * C * feats
    half = block // 2
    part = half // 2
    pad = -half % 128
    wide = half + pad
    x, y, z, c = (lax.axis_index(name) for name in ("x", "y", "z", "c"))

    partner = flip(weight, "c", C, 1)
    along = spread(hidden.T, "z", Z)
    along, partner = lax.optimization_barrier((along, partner))
    along = along.reshape(2, Z // 2, feats, rows)
    keep = lax.dynamic_index_in_dim(along, c, 0, keepdims=False)
    give = lax.dynamic_index_in_dim(along, 1 - c, 0, keepdims=False)
    got = flip(give, "c", C, 1)
    along = jnp.stack([jnp.where(c == 0, keep, got), jnp.where(c == 0, got, keep)], 1).reshape(half, rows)
    a, b = along[:part], jnp.concatenate([along[part:], digits(targets)])
    a, b = at_once(a, b)
    a1, b1 = at_once(flip(a, "y", Y, 1), flip(b, "x", X, 1))
    a01, b01 = jnp.stack([a, a1]), jnp.stack([b, b1])
    a32, b32 = at_once(flip(a01, "y", Y, 3), flip(b01, "x", X, 3))
    a2 = jnp.stack([a01[0], a01[1], a32[1], a32[0]])
    b2 = jnp.stack([b01[0], b01[1], b32[1], b32[0]])
    tgt = undigits(b2[:, part:]).reshape(X * rows)
    a2, b2 = at_once(a2, b2[:, :part])
    ax1, by1, ax3, by3 = at_once(flip(a2, "x", X, 1), flip(b2, "y", Y, 1), flip(a2, "x", X, 3), flip(b2, "y", Y, 3))
    ax2lo, by2lo = flip(ax1[: Y // 2], "x", X, 3), flip(by1[: X // 2], "y", Y, 3)
    ax2hi, by2hi = flip(ax3[Y // 2 :], "x", X, 1), flip(by3[X // 2 :], "y", Y, 1)
    ax2lo, by2lo, ax2hi, by2hi = at_once(ax2lo, by2lo, ax2hi, by2hi)
    places = jnp.stack([y ^ step for step in range(Y)])
    meta = jnp.append(places * block + c * (half - pad), c * pad)

    logits, theirs, ht = logits_of(
        meta, weight, partner, [a2, ax1, ax3, ax2lo, ax2hi], [b2, by1, by3, by2lo, by2hi], wide
    )
    logits = logits + flip(theirs, "c", C, 1)
    capped = CAP * jnp.tanh(logits / CAP)
    offset = (((x * Y + y) * Z + z) * C + c) * voc
    columns = offset + jnp.arange(voc, dtype=jnp.int32)
    hit = columns[:, None] == tgt[None, :]
    stats = jnp.stack([jnp.sum(jnp.exp(capped - CAP), 0), jnp.sum(jnp.where(hit, capped, 0.0), 0)])
    stats, ht, weight, partner = at_once(stats, ht, weight, partner)
    other = flip(ht, "c", C, 1)
    lows = [c * half, c * half + part]
    windows = [places * block + low // 128 * 128 for low in lows]
    meta = jnp.concatenate(windows + [jnp.stack([low % 128 for low in lows])])
    wt = turned_weights(meta, weight, partner, part, -(-part // 128) * 128)
    stats = spread(stats.reshape(2, X, rows), ("z", "c"), Z * C).sum(0)
    stats = reordered(stats, x, 1)
    stats, wt, other = at_once(stats, wt, other)
    stats = spread(stats, ("x", "y"), X * Y).sum(0)
    stats = reordered(stats, x, 1)
    lse = CAP + jnp.log(stats[0])
    loss = lse[0] - stats[1, 0]
    probs = jnp.exp(capped - lse.reshape(1, X * rows))
    dlogits = ((probs - hit.astype(F32)) * (1.0 - (capped / CAP) ** 2)).astype(BF16)

    dlo = flip(dlogits, "c", C, 1)
    a_half = jax.ShapeDtypeStruct((Y // 2, part, rows), BF16)
    b_half = jax.ShapeDtypeStruct((part // 2, X * rows), BF16)
    a_lo, a_hi, b_lo, b_hi = gradient_call(
        first_kernel, FIRST_BLOCKS, [a_half] * 2 + [b_half] * 2, wt, dlogits, dlo
    )
    a_lo, b_lo, a_hi, b_hi = at_once(
        flip(a_lo, "x", X, 1), flip(b_lo, "y", Y, 1), flip(a_hi, "x", X, 3), flip(b_hi, "y", Y, 3)
    )
    a_kind = jax.ShapeDtypeStruct((Y, part, rows), F32)
    b_kind = jax.ShapeDtypeStruct((part, X * rows), F32)
    a0, a1, a3, b0, b1, b3 = gradient_call(
        rest_kernel, REST_BLOCKS, [a_kind] * 3 + [b_kind] * 3, wt, dlogits, dlo
    )
    a1 = jnp.concatenate([a1[: Y // 2], a1[Y // 2 :] + a_hi.astype(F32)]).astype(BF16)
    a3 = jnp.concatenate([a3[: Y // 2] + a_lo.astype(F32), a3[Y // 2 :]]).astype(BF16)
    b1 = jnp.concatenate([b1[: part // 2], b1[part // 2 :] + b_hi.astype(F32)]).astype(BF16)
    b3 = jnp.concatenate([b3[: part // 2] + b_lo.astype(F32), b3[part // 2 :]]).astype(BF16)
    a1, b1, a3, b3 = at_once(a1, b1, a3, b3)
    a1, b1, a3, b3 = at_once(flip(a1, "x", X, 1), flip(b1, "y", Y, 1), flip(a3, "x", X, 3), flip(b3, "y", Y, 3))
    a_own = a0 + a1.astype(F32) + a3.astype(F32)
    b_own = b0 + b1.astype(F32) + b3.astype(F32)
    a_out, b_out = at_once(a_own[1:3].astype(BF16), b_own[:, rows : 3 * rows].astype(BF16))
    a_in, b_in = at_once(flip(a_out, "y", Y, 1), flip(b_out, "x", X, 1))
    a_out = (a_own[3] + a_in[1].astype(F32)).astype(BF16)
    b_out = (b_own[:, 3 * rows :] + b_in[:, rows:].astype(F32)).astype(BF16)
    a_out, b_out = at_once(a_out, b_out)
    a_out, b_out = at_once(flip(a_out, "y", Y, 3), flip(b_out, "x", X, 3))
    a_sum = a_own[0] + a_in[0].astype(F32) + a_out.astype(F32)
    b_sum = b_own[:, :rows] + b_in[:, :rows].astype(F32) + b_out.astype(F32)
    total = jnp.concatenate([a_sum, b_sum]).reshape(Z // 2, C, feats, rows)
    mine = lax.dynamic_index_in_dim(total, c, 1, keepdims=False)
    theirs = flip(lax.dynamic_index_in_dim(total, 1 - c, 1, keepdims=False), "c", C, 1)
    by_z = jnp.concatenate([jnp.where(c == 0, mine, theirs), jnp.where(c == 0, theirs, mine)])
    by_z, dlogits = lax.optimization_barrier((by_z, dlogits))
    grad_weight = weight_of(jnp.append(places, c), dlogits, ht, other)
    grad_hidden = lax.all_to_all(by_z, "z", 0, 0, tiled=True).sum(0).astype(BF16).T
    return loss, grad_hidden, grad_weight


def solution(mesh):
    chips = Mesh(mesh.devices.reshape(X, Y, Z, C), ("x", "y", "z", "c"))
    in_specs = (P("x", ("y", "z", "c")), P(("x", "y", "z", "c"), None), P("x"))
    out_specs = (P("x"), P("x", ("y", "z", "c")), P(("x", "y", "z", "c"), None))
    return jax.shard_map(per_device, mesh=chips, in_specs=in_specs, out_specs=out_specs, check_vma=False)
```

```python
import jax
import jax.numpy as jnp
from jax import lax
from jax.experimental import pallas as pl
from jax.experimental.pallas import tpu as pltpu
from jax.sharding import Mesh, PartitionSpec as P

CAP = 30
F32, BF16 = jnp.float32, jnp.bfloat16
X, Y, Z, C = 4, 4, 8, 2


def flip(array, axis, size, change):
    return lax.ppermute(array, axis, [(i, i ^ change) for i in range(size)])


def reordered(array, own, dim):
    return jnp.concatenate([lax.dynamic_slice_in_dim(array, own ^ k, 1, dim) for k in range(4)], dim)


def at_once(*arrays):
    return lax.optimization_barrier(arrays)


def spread(array, axes, size):
    copies = jnp.broadcast_to(array[None], (size,) + array.shape)
    return lax.all_to_all(copies, axes, 0, 0, tiled=True)


def digits(targets):
    parts = [targets // 65536, (targets // 256) % 256, targets % 256]
    return jnp.concatenate([jnp.stack(parts), jnp.zeros((5, targets.shape[0]), jnp.int32)]).astype(BF16)


def undigits(rows):
    parts = rows.astype(jnp.int32)
    return parts[:, 0] * 65536 + parts[:, 1] * 256 + parts[:, 2]


VMEM_LIMIT = 18 * 1024 * 1024


def start_all(copies):
    for copy in copies:
        copy.start()


def wait_all(copies):
    for copy in copies:
        copy.wait()


def in_hbm(arrays):
    return [pltpu.with_memory_space_constraint(array, pltpu.HBM) for array in arrays]


def logits_kernel(meta_ref, own_ref, other_ref, *refs):
    a_refs, b_refs = refs[:X], refs[X : X + Y]
    mine_ref, theirs_ref, ht_ref, slots, tall, sems, piece_sems, out_sem = refs[X + Y :]
    part, rows = a_refs[0].shape[1:]
    wide = tall.shape[1]
    shift = pl.multiple_of(meta_ref[Y], 64)
    pieces = []
    for place in range(X):
        target = tall.at[:, pl.ds(shift, part), pl.ds(place * rows, rows)]
        pieces.append(pltpu.make_async_copy(a_refs[place], target, piece_sems.at[Y, place]))
        for k in range(X):
            target = tall.at[place, pl.ds(shift + part, part), pl.ds(k * rows, rows)]
            pieces.append(pltpu.make_async_copy(b_refs[place].at[k], target, piece_sems.at[place, k]))
    start_all(pieces)
    halves = [[], []]
    for step in range(Y):
        columns = pl.ds(pl.multiple_of(meta_ref[step], 128), wide)
        for place, ref in enumerate((own_ref, other_ref)):
            target = slots.at[place, :, pl.ds(step * wide, wide)]
            copy = pltpu.make_async_copy(ref.at[:, columns], target, sems.at[step, place])
            halves[step // 2].append(copy)
    start_all(halves[0])
    edge = wide - 2 * part
    zeros = jnp.zeros((edge, X * rows), tall.dtype)
    empty = pl.multiple_of(2 * part * (1 - meta_ref[Y] // edge), 64)
    for step in range(Y):
        tall[step, pl.ds(empty, edge)] = zeros
    wait_all(pieces)
    wait_all(halves[0])
    start_all(halves[1])
    keep = pltpu.make_async_copy(tall.at[:, pl.ds(shift, 2 * part)], ht_ref, out_sem)
    depth = Y // 2 * wide
    for i, half in enumerate(halves):
        if i == 1:
            wait_all(half)
            keep.start()
        steps = tall[i * Y // 2 : (i + 1) * Y // 2].reshape(depth, X * rows)
        for place, out_ref in enumerate((mine_ref, theirs_ref)):
            term = jnp.dot(slots[place, :, i * depth : (i + 1) * depth], steps, preferred_element_type=F32)
            if i == 0:
                out_ref[...] = term
            else:
                out_ref[...] += term
    keep.wait()


def logits_of(meta, own, other, a_pieces, b_pieces, wide):
    voc = own.shape[0]
    part, rows = a_pieces[0].shape[1:]
    vmem = pl.BlockSpec(memory_space=pltpu.VMEM)
    hbm = pl.BlockSpec(memory_space=pltpu.HBM)
    square = pltpu.VMEM((voc, X * rows), F32)
    return pl.pallas_call(
        logits_kernel,
        out_shape=(square, square, pltpu.HBM((Y, 2 * part, X * rows), BF16)),
        in_specs=[pl.BlockSpec(memory_space=pltpu.SMEM), hbm, hbm] + [pl.BlockSpec(memory_space=pl.ANY)] * (X + Y),
        out_specs=(vmem, vmem, hbm),
        scratch_shapes=[
            pltpu.VMEM((2, voc, Y * wide), BF16),
            pltpu.VMEM((Y, wide, X * rows), BF16),
            pltpu.SemaphoreType.DMA((Y, 2)),
            pltpu.SemaphoreType.DMA((Y + 1, X)),
            pltpu.SemaphoreType.DMA,
        ],
        compiler_params=pltpu.CompilerParams(vmem_limit_bytes=VMEM_LIMIT),
        cost_estimate=pl.CostEstimate(
            flops=4 * Y * voc * wide * X * rows, bytes_accessed=4 * Y * voc * wide, transcendentals=0
        ),
    )(meta, *in_hbm([own, other]), *a_pieces, *b_pieces)


def turn_kernel(meta_ref, own_ref, other_ref, out_ref, slots, whole, made, sems, out_sems):
    part = out_ref.shape[2]
    voc, wide = slots.shape[2:]
    copies, outs = [], []
    for i in range(2 * Y):
        columns = pl.ds(pl.multiple_of(meta_ref[i], 128), wide)
        row = [
            pltpu.make_async_copy(ref.at[:, columns], slots.at[i, place], sems.at[i, place])
            for place, ref in enumerate((own_ref, other_ref))
        ]
        copies.append(row)
    for row in copies:
        for copy in row:
            copy.start()
    for i in range(2 * Y):
        shift = pl.multiple_of(meta_ref[2 * Y + i // Y], 32)
        for place in range(2):
            copies[i][place].wait()
            whole[i % 2, place] = slots[i, place].T
            made[i, :, place * voc : (place + 1) * voc] = whole[i % 2, place, pl.ds(shift, part)]
        out = pltpu.make_async_copy(made.at[i], out_ref.at[i % Y, i // Y], out_sems.at[i])
        out.start()
        outs.append(out)
    for out in outs:
        out.wait()


def turned_weights(meta, own, other, part, wide):
    voc = own.shape[0]
    hbm = pl.BlockSpec(memory_space=pltpu.HBM)
    return pl.pallas_call(
        turn_kernel,
        out_shape=pltpu.HBM((Y, 2, part, 2 * voc), BF16),
        in_specs=[pl.BlockSpec(memory_space=pltpu.SMEM), hbm, hbm],
        out_specs=hbm,
        scratch_shapes=[
            pltpu.VMEM((2 * Y, 2, voc, wide), BF16),
            pltpu.VMEM((2, 2, wide, voc), BF16),
            pltpu.VMEM((2 * Y, part, 2 * voc), BF16),
            pltpu.SemaphoreType.DMA((2 * Y, 2)),
            pltpu.SemaphoreType.DMA((2 * Y,)),
        ],
        compiler_params=pltpu.CompilerParams(vmem_limit_bytes=VMEM_LIMIT),
        cost_estimate=pl.CostEstimate(flops=0, bytes_accessed=12 * Y * voc * wide, transcendentals=0),
    )(meta, *in_hbm([own, other]))


FIRST_BLOCKS = ((0, 0), (1, 0), (2, 0), (3, 0), (2, 1))
REST_BLOCKS = ((0, 0), (1, 0), (2, 0), (3, 0), (0, 1), (1, 1), (3, 1))


def fetch_blocks(wt_ref, blocks, slots, sems):
    return [
        pltpu.make_async_copy(wt_ref.at[step, side], slots.at[i], sems.at[i]) for i, (step, side) in enumerate(blocks)
    ]


def product(slots, first, last, dls):
    blocks = slots[first:last].reshape((last - first) * slots.shape[1], slots.shape[2])
    return jnp.dot(blocks, dls, preferred_element_type=F32)


def first_kernel(base_ref, wt_ref, grown_ref, grown_other_ref, tgt_ref, vectors_ref, *refs):
    dls_ref, alo_ref, ahi_ref, blo_ref, bhi_ref, slots, sems = refs
    part, rows = alo_ref.shape[1:]
    copies = fetch_blocks(wt_ref, FIRST_BLOCKS, slots, sems)
    start_all(copies)
    chunk = 64
    voc = grown_ref.shape[0]
    for i, source_ref in enumerate((grown_ref, grown_other_ref)):
        for low in range(0, voc, chunk):
            columns = base_ref[i] + low + lax.broadcasted_iota(jnp.int32, (chunk, dls_ref.shape[1]), 0)
            value = source_ref[low : low + chunk] * vectors_ref[0:1]
            value = jnp.where(columns == tgt_ref[...], vectors_ref[1:2], value)
            dls_ref[i * voc + low : i * voc + low + chunk] = value.astype(BF16)
    wait_all(copies)
    a = product(slots, 0, Y, dls_ref[:, 2 * rows : 3 * rows]).astype(BF16)
    for step in range(Y):
        out_ref = alo_ref if step < Y // 2 else ahi_ref
        out_ref[step % (Y // 2)] = a[step * part : (step + 1) * part]
    b = product(slots, Y, Y + 1, dls_ref[...]).astype(BF16)
    blo_ref[...], bhi_ref[...] = b[: part // 2], b[part // 2 :]


def first_call(base, wt, grown, grown_other, tgt, vectors):
    vmem = pl.BlockSpec(memory_space=pltpu.VMEM)
    hbm = pl.BlockSpec(memory_space=pltpu.HBM)
    voc, all_rows = grown.shape
    part = wt.shape[2]
    dls = jax.ShapeDtypeStruct((2 * voc, all_rows), BF16)
    a_half = jax.ShapeDtypeStruct((Y // 2, part, all_rows // X), BF16)
    b_half = jax.ShapeDtypeStruct((part // 2, all_rows), BF16)
    count = len(FIRST_BLOCKS)
    return pl.pallas_call(
        first_kernel,
        out_shape=(dls, a_half, a_half, b_half, b_half),
        in_specs=[pl.BlockSpec(memory_space=pltpu.SMEM), hbm] + [vmem] * 4,
        out_specs=tuple([vmem] * 5),
        scratch_shapes=[
            pltpu.VMEM((count, part, 2 * voc), BF16),
            pltpu.SemaphoreType.DMA((count,)),
        ],
        compiler_params=pltpu.CompilerParams(vmem_limit_bytes=VMEM_LIMIT),
        cost_estimate=pl.CostEstimate(
            flops=2 * wt.size * all_rows // 4, bytes_accessed=wt.size + 8 * grown.size, transcendentals=0
        ),
    )(base, *in_hbm([wt]), grown, grown_other, tgt, vectors)


def rest_kernel(wt_ref, dls_ref, *refs):
    a_outs, b_outs = refs[:3], refs[3:6]
    slots, sems = refs[6:]
    part, rows = a_outs[0].shape[1:]
    copies = fetch_blocks(wt_ref, REST_BLOCKS, slots, sems)
    start_all(copies[:Y])
    wait_all(copies[:Y])
    start_all(copies[Y:])
    a = product(slots, 0, Y, dls_ref[...])
    for step in range(Y):
        for out_ref, place in zip(a_outs, (0, 1, 3)):
            out_ref[step] = a[step * part : (step + 1) * part, place * rows : (place + 1) * rows]
    wait_all(copies[Y:])
    b = product(slots, Y, Y + 3, dls_ref[...])
    for i, out_ref in enumerate(b_outs):
        out_ref[...] = b[i * part : (i + 1) * part]


def rest_call(outs, wt, dls):
    vmem = pl.BlockSpec(memory_space=pltpu.VMEM)
    part, wide = wt.shape[2:]
    count = len(REST_BLOCKS)
    return pl.pallas_call(
        rest_kernel,
        out_shape=tuple(outs),
        in_specs=[pl.BlockSpec(memory_space=pltpu.HBM), vmem],
        out_specs=tuple([vmem] * len(outs)),
        scratch_shapes=[pltpu.VMEM((count, part, wide), BF16), pltpu.SemaphoreType.DMA((count,))],
        compiler_params=pltpu.CompilerParams(vmem_limit_bytes=VMEM_LIMIT),
        cost_estimate=pl.CostEstimate(
            flops=2 * count * part * wide * dls.shape[1], bytes_accessed=2 * count * part * wide, transcendentals=0
        ),
    )(*in_hbm([wt]), dls)


def weight_kernel(places_ref, dl_ref, here_ref, there_ref, out_ref, both):
    half = here_ref.shape[1]
    core = places_ref[Y]
    both[pl.ds(pl.multiple_of(core * half, 64), half)] = here_ref[0]
    both[pl.ds(pl.multiple_of((1 - core) * half, 64), half)] = there_ref[0]
    over_last = (((1,), (1,)), ((), ()))
    out_ref[...] = lax.dot_general(dl_ref[...], both[...], over_last, preferred_element_type=F32).astype(BF16)


def weight_of(places, dls, here, there):
    voc, all_rows = dls.shape[0] // 2, dls.shape[1]
    half = here.shape[1]
    one = pl.BlockSpec((1, half, all_rows), lambda i, places: (i, 0, 0))
    return pl.pallas_call(
        weight_kernel,
        out_shape=jax.ShapeDtypeStruct((voc, Y * 2 * half), BF16),
        grid_spec=pltpu.PrefetchScalarGridSpec(
            num_scalar_prefetch=1,
            grid=(Y,),
            in_specs=[pl.BlockSpec((voc, all_rows), lambda i, places: (0, 0)), one, one],
            out_specs=pl.BlockSpec((voc, 2 * half), lambda i, places: (0, places[i])),
            scratch_shapes=[pltpu.VMEM((2 * half, all_rows), BF16)],
        ),
        compiler_params=pltpu.CompilerParams(vmem_limit_bytes=VMEM_LIMIT),
        cost_estimate=pl.CostEstimate(
            flops=4 * Y * voc * half * all_rows, bytes_accessed=8 * Y * half * all_rows, transcendentals=0
        ),
    )(places, dls, *in_hbm([here, there]))


def per_device(hidden, weight, targets):
    rows, feats = hidden.shape
    voc = weight.shape[0]
    block = Z * C * feats
    half = block // 2
    part = half // 2
    pad = -half % 128
    wide = half + pad
    x, y, z, c = (lax.axis_index(name) for name in ("x", "y", "z", "c"))

    partner = flip(weight, "c", C, 1)
    along = spread(hidden.T, "z", Z)
    places = jnp.stack([y ^ step for step in range(Y)])
    lows = [c * half, c * half + part]
    windows = [places * block + low // 128 * 128 for low in lows]
    meta = jnp.concatenate(windows + [jnp.stack([low % 128 for low in lows])])
    wt = turned_weights(meta, weight, partner, part, -(-part // 128) * 128)
    along, wt = at_once(along, wt)
    along = along.reshape(2, Z // 2, feats, rows)
    keep = lax.dynamic_index_in_dim(along, c, 0, keepdims=False)
    give = lax.dynamic_index_in_dim(along, 1 - c, 0, keepdims=False)
    got = flip(give, "c", C, 1)
    along = jnp.stack([jnp.where(c == 0, keep, got), jnp.where(c == 0, got, keep)], 1).reshape(half, rows)
    a, b = along[:part], jnp.concatenate([along[part:], digits(targets)])
    a, b = at_once(a, b)
    a1, b1 = at_once(flip(a, "y", Y, 1), flip(b, "x", X, 1))
    a01, b01 = jnp.stack([a, a1]), jnp.stack([b, b1])
    a32, b32 = at_once(flip(a01, "y", Y, 3), flip(b01, "x", X, 3))
    a2 = jnp.stack([a01[0], a01[1], a32[1], a32[0]])
    b2 = jnp.stack([b01[0], b01[1], b32[1], b32[0]])
    tgt = undigits(b2[:, part:]).reshape(X * rows)
    a2, b2 = at_once(a2, b2[:, :part])
    ax1, by1, ax3, by3, ax2, by2 = at_once(
        *[flip(array, axis, 4, step) for step in (1, 3, 2) for array, axis in ((a2, "x"), (b2, "y"))]
    )
    meta = jnp.append(places * block + c * (half - pad), c * pad)

    mine, theirs, ht = logits_of(
        meta, weight, partner, [a2, ax1, ax2, ax3], [b2, by1, by2, by3], wide
    )
    theirs = flip(theirs, "c", C, 1)
    capped = CAP * jnp.tanh((mine + theirs) / CAP)
    offset = (((x * Y + y) * Z + z) * C + c) * voc
    columns = offset + jnp.arange(voc, dtype=jnp.int32)
    hit = columns[:, None] == tgt[None, :]
    stats = jnp.stack([jnp.sum(jnp.exp(capped - CAP), 0), jnp.sum(jnp.where(hit, capped, 0.0), 0)])
    stats, ht, mine, theirs = at_once(stats, ht, mine, theirs)
    other = flip(ht, "c", C, 1)
    capped = CAP * jnp.tanh((mine + theirs) / CAP)
    grown = jnp.exp(capped - CAP) * (1.0 - (capped / CAP) ** 2)
    stats = spread(stats.reshape(2, X, rows), ("z", "c"), Z * C).sum(0)
    stats = reordered(stats, x, 1)
    stats, grown, other = at_once(stats, grown, other)
    grown_other = flip(grown, "c", C, 1)
    stats = spread(stats, ("x", "y"), X * Y).sum(0)
    stats = reordered(stats, x, 1)
    stats, grown_other = at_once(stats, grown_other)
    lse = CAP + jnp.log(stats[0])
    loss = lse[0] - stats[1, 0]
    at_target = (jnp.exp(stats[1] - lse) - 1.0) * (1.0 - (stats[1] / CAP) ** 2)
    vectors = jnp.stack([(1.0 / stats[0]).reshape(-1), at_target.reshape(-1)])
    base = jnp.stack([offset, offset + (1 - 2 * c) * voc])

    dls, a_lo, a_hi, b_lo, b_hi = first_call(base, wt, grown, grown_other, tgt[None], vectors)
    a_lo, b_lo, a_hi, b_hi = at_once(
        flip(a_lo, "x", X, 1), flip(b_lo, "y", Y, 1), flip(a_hi, "x", X, 3), flip(b_hi, "y", Y, 3)
    )
    a_kind = jax.ShapeDtypeStruct((Y, part, rows), F32)
    b_kind = jax.ShapeDtypeStruct((part, X * rows), F32)
    a0, a1, a3, b0, b1, b3 = rest_call([a_kind] * 3 + [b_kind] * 3, wt, dls)
    a1 = jnp.concatenate([a1[: Y // 2], a1[Y // 2 :] + a_hi.astype(F32)]).astype(BF16)
    a3 = jnp.concatenate([a3[: Y // 2] + a_lo.astype(F32), a3[Y // 2 :]]).astype(BF16)
    b1 = jnp.concatenate([b1[: part // 2], b1[part // 2 :] + b_hi.astype(F32)]).astype(BF16)
    b3 = jnp.concatenate([b3[: part // 2] + b_lo.astype(F32), b3[part // 2 :]]).astype(BF16)
    a1, b1, a3, b3 = at_once(a1, b1, a3, b3)
    a1, b1, a3, b3 = at_once(flip(a1, "x", X, 1), flip(b1, "y", Y, 1), flip(a3, "x", X, 3), flip(b3, "y", Y, 3))
    a_own = a0 + a1.astype(F32) + a3.astype(F32)
    b_own = b0 + b1.astype(F32) + b3.astype(F32)
    a_out, b_out = at_once(a_own[1:3].astype(BF16), b_own[:, rows : 3 * rows].astype(BF16))
    a_in, b_in = at_once(flip(a_out, "y", Y, 1), flip(b_out, "x", X, 1))
    a_out = (a_own[3] + a_in[1].astype(F32)).astype(BF16)
    b_out = (b_own[:, 3 * rows :] + b_in[:, rows:].astype(F32)).astype(BF16)
    a_out, b_out = at_once(a_out, b_out)
    a_out, b_out = at_once(flip(a_out, "y", Y, 3), flip(b_out, "x", X, 3))
    a_sum = a_own[0] + a_in[0].astype(F32) + a_out.astype(F32)
    b_sum = b_own[:, :rows] + b_in[:, :rows].astype(F32) + b_out.astype(F32)
    total = jnp.concatenate([a_sum, b_sum]).reshape(Z // 2, C, feats, rows)
    mine = lax.dynamic_index_in_dim(total, c, 1, keepdims=False)
    theirs = flip(lax.dynamic_index_in_dim(total, 1 - c, 1, keepdims=False), "c", C, 1)
    by_z = jnp.concatenate([jnp.where(c == 0, mine, theirs), jnp.where(c == 0, theirs, mine)])
    by_z, dls = at_once(by_z, dls)
    grad_weight = weight_of(jnp.append(places, c), dls, ht, other)
    grad_hidden = lax.all_to_all(by_z, "z", 0, 0, tiled=True).sum(0).astype(BF16).T
    return loss, grad_hidden, grad_weight


def solution(mesh):
    chips = Mesh(mesh.devices.reshape(X, Y, Z, C), ("x", "y", "z", "c"))
    in_specs = (P("x", ("y", "z", "c")), P(("x", "y", "z", "c"), None), P("x"))
    out_specs = (P("x"), P("x", ("y", "z", "c")), P(("x", "y", "z", "c"), None))
    return jax.shard_map(per_device, mesh=chips, in_specs=in_specs, out_specs=out_specs, check_vma=False)
```

```python
import jax
import jax.numpy as jnp
from jax import lax
from jax.experimental import pallas as pl
from jax.experimental.pallas import tpu as pltpu
from jax.sharding import Mesh, PartitionSpec as P

CAP = 30
F32, BF16 = jnp.float32, jnp.bfloat16
X, Y, Z, C = 4, 4, 8, 2


def flip(array, axis, size, change):
    return lax.ppermute(array, axis, [(i, i ^ change) for i in range(size)])


def reordered(array, own, dim):
    return jnp.concatenate([lax.dynamic_slice_in_dim(array, own ^ k, 1, dim) for k in range(4)], dim)


def at_once(*arrays):
    return lax.optimization_barrier(arrays)


def spread(array, axes, size):
    copies = jnp.broadcast_to(array[None], (size,) + array.shape)
    return lax.all_to_all(copies, axes, 0, 0, tiled=True)


def digits(targets):
    parts = [targets // 65536, (targets // 256) % 256, targets % 256]
    return jnp.concatenate([jnp.stack(parts), jnp.zeros((5, targets.shape[0]), jnp.int32)]).astype(BF16)


def undigits(rows):
    parts = rows.astype(jnp.int32)
    return parts[:, 0] * 65536 + parts[:, 1] * 256 + parts[:, 2]


VMEM_LIMIT = 18 * 1024 * 1024


def start_all(copies):
    for copy in copies:
        copy.start()


def wait_all(copies):
    for copy in copies:
        copy.wait()


def in_hbm(arrays):
    return [pltpu.with_memory_space_constraint(array, pltpu.HBM) for array in arrays]


def logits_kernel(meta_ref, own_ref, other_ref, *refs):
    a_refs, b_refs = refs[:X], refs[X : X + Y]
    mine_ref, theirs_ref, ht_ref, slots, tall, sems, piece_sems, out_sem = refs[X + Y :]
    part, rows = a_refs[0].shape[1:]
    wide = tall.shape[1]
    shift = pl.multiple_of(meta_ref[Y], 64)
    pieces = []
    for place in range(X):
        target = tall.at[:, pl.ds(shift, part), pl.ds(place * rows, rows)]
        pieces.append(pltpu.make_async_copy(a_refs[place], target, piece_sems.at[Y, place]))
        for k in range(X):
            target = tall.at[place, pl.ds(shift + part, part), pl.ds(k * rows, rows)]
            pieces.append(pltpu.make_async_copy(b_refs[place].at[k], target, piece_sems.at[place, k]))
    start_all(pieces)
    halves = [[], []]
    for step in range(Y):
        columns = pl.ds(pl.multiple_of(meta_ref[step], 128), wide)
        for place, ref in enumerate((own_ref, other_ref)):
            target = slots.at[place, :, pl.ds(step * wide, wide)]
            copy = pltpu.make_async_copy(ref.at[:, columns], target, sems.at[step, place])
            halves[step // 2].append(copy)
    start_all(halves[0])
    edge = wide - 2 * part
    zeros = jnp.zeros((edge, X * rows), tall.dtype)
    empty = pl.multiple_of(2 * part * (1 - meta_ref[Y] // edge), 64)
    for step in range(Y):
        tall[step, pl.ds(empty, edge)] = zeros
    wait_all(pieces)
    wait_all(halves[0])
    start_all(halves[1])
    keep = pltpu.make_async_copy(tall.at[:, pl.ds(shift, 2 * part)], ht_ref, out_sem)
    depth = Y // 2 * wide
    for i, half in enumerate(halves):
        if i == 1:
            wait_all(half)
            keep.start()
        steps = tall[i * Y // 2 : (i + 1) * Y // 2].reshape(depth, X * rows)
        for place, out_ref in enumerate((mine_ref, theirs_ref)):
            term = jnp.dot(slots[place, :, i * depth : (i + 1) * depth], steps, preferred_element_type=F32)
            if i == 0:
                out_ref[...] = term
            else:
                out_ref[...] += term
    keep.wait()


def logits_of(meta, own, other, a_pieces, b_pieces, wide):
    voc = own.shape[0]
    part, rows = a_pieces[0].shape[1:]
    vmem = pl.BlockSpec(memory_space=pltpu.VMEM)
    hbm = pl.BlockSpec(memory_space=pltpu.HBM)
    square = pltpu.VMEM((voc, X * rows), F32)
    return pl.pallas_call(
        logits_kernel,
        out_shape=(square, square, pltpu.HBM((Y, 2 * part, X * rows), BF16)),
        in_specs=[pl.BlockSpec(memory_space=pltpu.SMEM), hbm, hbm] + [pl.BlockSpec(memory_space=pl.ANY)] * (X + Y),
        out_specs=(vmem, vmem, hbm),
        scratch_shapes=[
            pltpu.VMEM((2, voc, Y * wide), BF16),
            pltpu.VMEM((Y, wide, X * rows), BF16),
            pltpu.SemaphoreType.DMA((Y, 2)),
            pltpu.SemaphoreType.DMA((Y + 1, X)),
            pltpu.SemaphoreType.DMA,
        ],
        compiler_params=pltpu.CompilerParams(vmem_limit_bytes=VMEM_LIMIT),
        cost_estimate=pl.CostEstimate(
            flops=4 * Y * voc * wide * X * rows, bytes_accessed=4 * Y * voc * wide, transcendentals=0
        ),
    )(meta, *in_hbm([own, other]), *a_pieces, *b_pieces)


def turn_kernel(meta_ref, own_ref, other_ref, out_ref, slots, whole, made, sems, out_sems):
    part = out_ref.shape[2]
    voc, wide = slots.shape[2:]
    copies, outs = [], []
    for i in range(2 * Y):
        columns = pl.ds(pl.multiple_of(meta_ref[i], 128), wide)
        row = [
            pltpu.make_async_copy(ref.at[:, columns], slots.at[i, place], sems.at[i, place])
            for place, ref in enumerate((own_ref, other_ref))
        ]
        copies.append(row)
    for row in copies:
        for copy in row:
            copy.start()
    for i in range(2 * Y):
        shift = pl.multiple_of(meta_ref[2 * Y + i // Y], 32)
        for place in range(2):
            copies[i][place].wait()
            whole[i % 2, place] = slots[i, place].T
            made[i, :, place * voc : (place + 1) * voc] = whole[i % 2, place, pl.ds(shift, part)]
        out = pltpu.make_async_copy(made.at[i], out_ref.at[i % Y, i // Y], out_sems.at[i])
        out.start()
        outs.append(out)
    for out in outs:
        out.wait()


def turned_weights(meta, own, other, part, wide):
    voc = own.shape[0]
    hbm = pl.BlockSpec(memory_space=pltpu.HBM)
    return pl.pallas_call(
        turn_kernel,
        out_shape=pltpu.HBM((Y, 2, part, 2 * voc), BF16),
        in_specs=[pl.BlockSpec(memory_space=pltpu.SMEM), hbm, hbm],
        out_specs=hbm,
        scratch_shapes=[
            pltpu.VMEM((2 * Y, 2, voc, wide), BF16),
            pltpu.VMEM((2, 2, wide, voc), BF16),
            pltpu.VMEM((2 * Y, part, 2 * voc), BF16),
            pltpu.SemaphoreType.DMA((2 * Y, 2)),
            pltpu.SemaphoreType.DMA((2 * Y,)),
        ],
        compiler_params=pltpu.CompilerParams(vmem_limit_bytes=VMEM_LIMIT),
        cost_estimate=pl.CostEstimate(flops=0, bytes_accessed=12 * Y * voc * wide, transcendentals=0),
    )(meta, *in_hbm([own, other]))


FIRST_BLOCKS = ((0, 0), (1, 0), (2, 0), (3, 0), (2, 1))
REST_BLOCKS = ((0, 0), (1, 0), (2, 0), (3, 0), (0, 1), (1, 1), (3, 1))


def fetch_blocks(wt_ref, blocks, slots, sems):
    return [
        pltpu.make_async_copy(wt_ref.at[step, side], slots.at[i], sems.at[i]) for i, (step, side) in enumerate(blocks)
    ]


def product(slots, first, last, dls):
    blocks = slots[first:last].reshape((last - first) * slots.shape[1], slots.shape[2])
    return jnp.dot(blocks, dls, preferred_element_type=F32)


def first_kernel(base_ref, wt_ref, grown_ref, grown_other_ref, tgt_ref, vectors_ref, *refs):
    dls_ref, a_ref, b_ref, slots, sems = refs
    part, rows = a_ref.shape[1:]
    copies = fetch_blocks(wt_ref, FIRST_BLOCKS, slots, sems)
    start_all(copies)
    chunk = 64
    voc = grown_ref.shape[0]
    for i, source_ref in enumerate((grown_ref, grown_other_ref)):
        for low in range(0, voc, chunk):
            columns = base_ref[i] + low + lax.broadcasted_iota(jnp.int32, (chunk, dls_ref.shape[1]), 0)
            value = source_ref[low : low + chunk] * vectors_ref[0:1]
            value = jnp.where(columns == tgt_ref[...], vectors_ref[1:2], value)
            dls_ref[i * voc + low : i * voc + low + chunk] = value.astype(BF16)
    wait_all(copies)
    a = product(slots, 0, Y, dls_ref[:, 2 * rows : 3 * rows]).astype(BF16)
    for step in range(Y):
        a_ref[step] = a[step * part : (step + 1) * part]
    b_ref[...] = product(slots, Y, Y + 1, dls_ref[...]).astype(BF16)


def first_call(base, wt, grown, grown_other, tgt, vectors):
    vmem = pl.BlockSpec(memory_space=pltpu.VMEM)
    hbm = pl.BlockSpec(memory_space=pltpu.HBM)
    voc, all_rows = grown.shape
    part = wt.shape[2]
    dls = jax.ShapeDtypeStruct((2 * voc, all_rows), BF16)
    a_far = jax.ShapeDtypeStruct((Y, part, all_rows // X), BF16)
    b_far = jax.ShapeDtypeStruct((part, all_rows), BF16)
    count = len(FIRST_BLOCKS)
    return pl.pallas_call(
        first_kernel,
        out_shape=(dls, a_far, b_far),
        in_specs=[pl.BlockSpec(memory_space=pltpu.SMEM), hbm] + [vmem] * 4,
        out_specs=(vmem,) * 3,
        scratch_shapes=[
            pltpu.VMEM((count, part, 2 * voc), BF16),
            pltpu.SemaphoreType.DMA((count,)),
        ],
        compiler_params=pltpu.CompilerParams(vmem_limit_bytes=VMEM_LIMIT),
        cost_estimate=pl.CostEstimate(
            flops=2 * wt.size * all_rows // 4, bytes_accessed=wt.size + 8 * grown.size, transcendentals=0
        ),
    )(base, *in_hbm([wt]), grown, grown_other, tgt, vectors)


def rest_kernel(wt_ref, dls_ref, *refs):
    a_outs, b_outs = refs[:3], refs[3:6]
    slots, sems = refs[6:]
    part, rows = a_outs[0].shape[1:]
    copies = fetch_blocks(wt_ref, REST_BLOCKS, slots, sems)
    start_all(copies[:Y])
    wait_all(copies[:Y])
    start_all(copies[Y:])
    a = product(slots, 0, Y, dls_ref[...])
    for step in range(Y):
        for out_ref, place in zip(a_outs, (0, 1, 3)):
            out_ref[step] = a[step * part : (step + 1) * part, place * rows : (place + 1) * rows]
    wait_all(copies[Y:])
    b = product(slots, Y, Y + 3, dls_ref[...])
    for i, out_ref in enumerate(b_outs):
        out_ref[...] = b[i * part : (i + 1) * part]


def rest_call(outs, wt, dls):
    vmem = pl.BlockSpec(memory_space=pltpu.VMEM)
    part, wide = wt.shape[2:]
    count = len(REST_BLOCKS)
    return pl.pallas_call(
        rest_kernel,
        out_shape=tuple(outs),
        in_specs=[pl.BlockSpec(memory_space=pltpu.HBM), vmem],
        out_specs=tuple([vmem] * len(outs)),
        scratch_shapes=[pltpu.VMEM((count, part, wide), BF16), pltpu.SemaphoreType.DMA((count,))],
        compiler_params=pltpu.CompilerParams(vmem_limit_bytes=VMEM_LIMIT),
        cost_estimate=pl.CostEstimate(
            flops=2 * count * part * wide * dls.shape[1], bytes_accessed=2 * count * part * wide, transcendentals=0
        ),
    )(*in_hbm([wt]), dls)


def weight_kernel(places_ref, dl_ref, here_ref, there_ref, out_ref, both):
    half = here_ref.shape[1]
    core = places_ref[Y]
    both[pl.ds(pl.multiple_of(core * half, 64), half)] = here_ref[0]
    both[pl.ds(pl.multiple_of((1 - core) * half, 64), half)] = there_ref[0]
    over_last = (((1,), (1,)), ((), ()))
    out_ref[...] = lax.dot_general(dl_ref[...], both[...], over_last, preferred_element_type=F32).astype(BF16)


def weight_of(places, dls, here, there):
    voc, all_rows = dls.shape[0] // 2, dls.shape[1]
    half = here.shape[1]
    one = pl.BlockSpec((1, half, all_rows), lambda i, places: (i, 0, 0))
    return pl.pallas_call(
        weight_kernel,
        out_shape=jax.ShapeDtypeStruct((voc, Y * 2 * half), BF16),
        grid_spec=pltpu.PrefetchScalarGridSpec(
            num_scalar_prefetch=1,
            grid=(Y,),
            in_specs=[pl.BlockSpec((voc, all_rows), lambda i, places: (0, 0)), one, one],
            out_specs=pl.BlockSpec((voc, 2 * half), lambda i, places: (0, places[i])),
            scratch_shapes=[pltpu.VMEM((2 * half, all_rows), BF16)],
        ),
        compiler_params=pltpu.CompilerParams(vmem_limit_bytes=VMEM_LIMIT),
        cost_estimate=pl.CostEstimate(
            flops=4 * Y * voc * half * all_rows, bytes_accessed=8 * Y * half * all_rows, transcendentals=0
        ),
    )(places, dls, *in_hbm([here, there]))


def per_device(hidden, weight, targets):
    rows, feats = hidden.shape
    voc = weight.shape[0]
    block = Z * C * feats
    half = block // 2
    part = half // 2
    pad = -half % 128
    wide = half + pad
    x, y, z, c = (lax.axis_index(name) for name in ("x", "y", "z", "c"))

    partner = flip(weight, "c", C, 1)
    along = spread(hidden.T, "z", Z)
    places = jnp.stack([y ^ step for step in range(Y)])
    lows = [c * half, c * half + part]
    windows = [places * block + low // 128 * 128 for low in lows]
    meta = jnp.concatenate(windows + [jnp.stack([low % 128 for low in lows])])
    wt = turned_weights(meta, weight, partner, part, -(-part // 128) * 128)
    along, wt = at_once(along, wt)
    along = along.reshape(2, Z // 2, feats, rows)
    keep = lax.dynamic_index_in_dim(along, c, 0, keepdims=False)
    give = lax.dynamic_index_in_dim(along, 1 - c, 0, keepdims=False)
    got = flip(give, "c", C, 1)
    along = jnp.stack([jnp.where(c == 0, keep, got), jnp.where(c == 0, got, keep)], 1).reshape(half, rows)
    a, b = along[:part], jnp.concatenate([along[part:], digits(targets)])
    a, b = at_once(a, b)
    a1, b1 = at_once(flip(a, "y", Y, 1), flip(b, "x", X, 1))
    a01, b01 = jnp.stack([a, a1]), jnp.stack([b, b1])
    a32, b32 = at_once(flip(a01, "y", Y, 3), flip(b01, "x", X, 3))
    a2 = jnp.stack([a01[0], a01[1], a32[1], a32[0]])
    b2 = jnp.stack([b01[0], b01[1], b32[1], b32[0]])
    tgt = undigits(b2[:, part:]).reshape(X * rows)
    a2, b2 = at_once(a2, b2[:, :part])
    ax1, by1, ax3, by3, ax2, by2 = at_once(
        *[flip(array, axis, 4, step) for step in (1, 3, 2) for array, axis in ((a2, "x"), (b2, "y"))]
    )
    meta = jnp.append(places * block + c * (half - pad), c * pad)

    mine, theirs, ht = logits_of(
        meta, weight, partner, [a2, ax1, ax2, ax3], [b2, by1, by2, by3], wide
    )
    theirs = flip(theirs, "c", C, 1)
    capped = CAP * jnp.tanh((mine + theirs) / CAP)
    offset = (((x * Y + y) * Z + z) * C + c) * voc
    columns = offset + jnp.arange(voc, dtype=jnp.int32)
    hit = columns[:, None] == tgt[None, :]
    stats = jnp.stack([jnp.sum(jnp.exp(capped - CAP), 0), jnp.sum(jnp.where(hit, capped, 0.0), 0)])
    stats, ht, mine, theirs = at_once(stats, ht, mine, theirs)
    other = flip(ht, "c", C, 1)
    capped = CAP * jnp.tanh((mine + theirs) / CAP)
    grown = jnp.exp(capped - CAP) * (1.0 - (capped / CAP) ** 2)
    stats = spread(stats.reshape(2, X, rows), ("z", "c"), Z * C).sum(0)
    stats = reordered(stats, x, 1)
    stats, grown, other = at_once(stats, grown, other)
    grown_other = flip(grown, "c", C, 1)
    stats = spread(stats, ("x", "y"), X * Y).sum(0)
    stats = reordered(stats, x, 1)
    stats, grown_other = at_once(stats, grown_other)
    lse = CAP + jnp.log(stats[0])
    loss = lse[0] - stats[1, 0]
    at_target = (jnp.exp(stats[1] - lse) - 1.0) * (1.0 - (stats[1] / CAP) ** 2)
    vectors = jnp.stack([(1.0 / stats[0]).reshape(-1), at_target.reshape(-1)])
    base = jnp.stack([offset, offset + (1 - 2 * c) * voc])

    dls, a_far, b_far = first_call(base, wt, grown, grown_other, tgt[None], vectors)
    a_far, b_far = at_once(flip(a_far, "x", X, 1), flip(b_far, "y", Y, 1))
    a_kind = jax.ShapeDtypeStruct((Y, part, rows), F32)
    b_kind = jax.ShapeDtypeStruct((part, X * rows), F32)
    a0, a1, a3, b0, b1, b3 = rest_call([a_kind] * 3 + [b_kind] * 3, wt, dls)
    a1, a3 = a1.astype(BF16), (a3 + a_far.astype(F32)).astype(BF16)
    b1, b3 = b1.astype(BF16), (b3 + b_far.astype(F32)).astype(BF16)
    a1, b1, a3, b3 = at_once(a1, b1, a3, b3)
    a1, b1, a3, b3 = at_once(flip(a1, "x", X, 1), flip(b1, "y", Y, 1), flip(a3, "x", X, 3), flip(b3, "y", Y, 3))
    a_own = a0 + a1.astype(F32) + a3.astype(F32)
    b_own = b0 + b1.astype(F32) + b3.astype(F32)
    a_out, b_out = at_once(a_own[1:3].astype(BF16), b_own[:, rows : 3 * rows].astype(BF16))
    a_in, b_in = at_once(flip(a_out, "y", Y, 1), flip(b_out, "x", X, 1))
    a_out = (a_own[3] + a_in[1].astype(F32)).astype(BF16)
    b_out = (b_own[:, 3 * rows :] + b_in[:, rows:].astype(F32)).astype(BF16)
    a_out, b_out = at_once(a_out, b_out)
    a_out, b_out = at_once(flip(a_out, "y", Y, 3), flip(b_out, "x", X, 3))
    a_sum = a_own[0] + a_in[0].astype(F32) + a_out.astype(F32)
    b_sum = b_own[:, :rows] + b_in[:, :rows].astype(F32) + b_out.astype(F32)
    total = jnp.concatenate([a_sum, b_sum]).reshape(Z // 2, C, feats, rows)
    mine = lax.dynamic_index_in_dim(total, c, 1, keepdims=False)
    theirs = flip(lax.dynamic_index_in_dim(total, 1 - c, 1, keepdims=False), "c", C, 1)
    by_z = jnp.concatenate([jnp.where(c == 0, mine, theirs), jnp.where(c == 0, theirs, mine)])
    by_z, dls = at_once(by_z, dls)
    grad_weight = weight_of(jnp.append(places, c), dls, ht, other)
    grad_hidden = lax.all_to_all(by_z, "z", 0, 0, tiled=True).sum(0).astype(BF16).T
    return loss, grad_hidden, grad_weight


def solution(mesh):
    chips = Mesh(mesh.devices.reshape(X, Y, Z, C), ("x", "y", "z", "c"))
    in_specs = (P("x", ("y", "z", "c")), P(("x", "y", "z", "c"), None), P("x"))
    out_specs = (P("x"), P("x", ("y", "z", "c")), P(("x", "y", "z", "c"), None))
    return jax.shard_map(per_device, mesh=chips, in_specs=in_specs, out_specs=out_specs, check_vma=False)
```

```python
import jax
import jax.numpy as jnp
from jax import lax
from jax.experimental import pallas as pl
from jax.experimental.pallas import tpu as pltpu
from jax.sharding import Mesh, PartitionSpec as P

CAP = 30
F32, BF16 = jnp.float32, jnp.bfloat16
X, Y, Z, C = 4, 4, 8, 2


def flip(array, axis, size, change):
    return lax.ppermute(array, axis, [(i, i ^ change) for i in range(size)])


def reordered(array, own, dim):
    return jnp.concatenate([lax.dynamic_slice_in_dim(array, own ^ k, 1, dim) for k in range(4)], dim)


def at_once(*arrays):
    return lax.optimization_barrier(arrays)


def spread(array, axes, size):
    copies = jnp.broadcast_to(array[None], (size,) + array.shape)
    return lax.all_to_all(copies, axes, 0, 0, tiled=True)


def digits(targets):
    parts = [targets // 65536, (targets // 256) % 256, targets % 256]
    return jnp.concatenate([jnp.stack(parts), jnp.zeros((5, targets.shape[0]), jnp.int32)]).astype(BF16)


def undigits(rows):
    parts = rows.astype(jnp.int32)
    return parts[:, 0] * 65536 + parts[:, 1] * 256 + parts[:, 2]


VMEM_LIMIT = 18 * 1024 * 1024


def start_all(copies):
    for copy in copies:
        copy.start()


def wait_all(copies):
    for copy in copies:
        copy.wait()


def in_hbm(arrays):
    return [pltpu.with_memory_space_constraint(array, pltpu.HBM) for array in arrays]


def logits_kernel(meta_ref, own_ref, other_ref, *refs):
    a_refs, b_refs = refs[:X], refs[X : X + Y]
    mine_ref, theirs_ref, ht_ref, slots, tall, sems, piece_sems, out_sem = refs[X + Y :]
    part, rows = a_refs[0].shape[1:]
    wide = tall.shape[1]
    shift = pl.multiple_of(meta_ref[Y], 64)
    pieces = []
    for place in range(X):
        target = tall.at[:, pl.ds(shift, part), pl.ds(place * rows, rows)]
        pieces.append(pltpu.make_async_copy(a_refs[place], target, piece_sems.at[Y, place]))
        for k in range(X):
            target = tall.at[place, pl.ds(shift + part, part), pl.ds(k * rows, rows)]
            pieces.append(pltpu.make_async_copy(b_refs[place].at[k], target, piece_sems.at[place, k]))
    start_all(pieces)
    halves = [[], []]
    for step in range(Y):
        columns = pl.ds(pl.multiple_of(meta_ref[step], 128), wide)
        for place, ref in enumerate((own_ref, other_ref)):
            target = slots.at[place, :, pl.ds(step * wide, wide)]
            copy = pltpu.make_async_copy(ref.at[:, columns], target, sems.at[step, place])
            halves[step // 2].append(copy)
    start_all(halves[0])
    edge = wide - 2 * part
    zeros = jnp.zeros((edge, X * rows), tall.dtype)
    empty = pl.multiple_of(2 * part * (1 - meta_ref[Y] // edge), 64)
    for step in range(Y):
        tall[step, pl.ds(empty, edge)] = zeros
    wait_all(pieces)
    wait_all(halves[0])
    start_all(halves[1])
    keep = pltpu.make_async_copy(tall.at[:, pl.ds(shift, 2 * part)], ht_ref, out_sem)
    depth = Y // 2 * wide
    for i, half in enumerate(halves):
        if i == 1:
            wait_all(half)
            keep.start()
        steps = tall[i * Y // 2 : (i + 1) * Y // 2].reshape(depth, X * rows)
        for place, out_ref in enumerate((mine_ref, theirs_ref)):
            term = jnp.dot(slots[place, :, i * depth : (i + 1) * depth], steps, preferred_element_type=F32)
            if i == 0:
                out_ref[...] = term
            else:
                out_ref[...] += term
    keep.wait()


def logits_of(meta, own, other, a_pieces, b_pieces, wide):
    voc = own.shape[0]
    part, rows = a_pieces[0].shape[1:]
    vmem = pl.BlockSpec(memory_space=pltpu.VMEM)
    hbm = pl.BlockSpec(memory_space=pltpu.HBM)
    square = pltpu.VMEM((voc, X * rows), F32)
    return pl.pallas_call(
        logits_kernel,
        out_shape=(square, square, pltpu.HBM((Y, 2 * part, X * rows), BF16)),
        in_specs=[pl.BlockSpec(memory_space=pltpu.SMEM), hbm, hbm] + [pl.BlockSpec(memory_space=pl.ANY)] * (X + Y),
        out_specs=(vmem, vmem, hbm),
        scratch_shapes=[
            pltpu.VMEM((2, voc, Y * wide), BF16),
            pltpu.VMEM((Y, wide, X * rows), BF16),
            pltpu.SemaphoreType.DMA((Y, 2)),
            pltpu.SemaphoreType.DMA((Y + 1, X)),
            pltpu.SemaphoreType.DMA,
        ],
        compiler_params=pltpu.CompilerParams(vmem_limit_bytes=VMEM_LIMIT),
        cost_estimate=pl.CostEstimate(
            flops=4 * Y * voc * wide * X * rows, bytes_accessed=4 * Y * voc * wide, transcendentals=0
        ),
    )(meta, *in_hbm([own, other]), *a_pieces, *b_pieces)


def turn_kernel(meta_ref, own_ref, other_ref, out_ref, slots, whole, made, sems, out_sems):
    part = out_ref.shape[2]
    voc, wide = slots.shape[2:]
    copies, outs = [], []
    for i in range(2 * Y):
        columns = pl.ds(pl.multiple_of(meta_ref[i], 128), wide)
        row = [
            pltpu.make_async_copy(ref.at[:, columns], slots.at[i, place], sems.at[i, place])
            for place, ref in enumerate((own_ref, other_ref))
        ]
        copies.append(row)
    for row in copies:
        for copy in row:
            copy.start()
    for i in range(2 * Y):
        shift = pl.multiple_of(meta_ref[2 * Y + i // Y], 32)
        for place in range(2):
            copies[i][place].wait()
            whole[i % 2, place] = slots[i, place].T
            made[i, :, place * voc : (place + 1) * voc] = whole[i % 2, place, pl.ds(shift, part)]
        out = pltpu.make_async_copy(made.at[i], out_ref.at[i % Y, i // Y], out_sems.at[i])
        out.start()
        outs.append(out)
    for out in outs:
        out.wait()


def turned_weights(meta, own, other, part, wide):
    voc = own.shape[0]
    hbm = pl.BlockSpec(memory_space=pltpu.HBM)
    return pl.pallas_call(
        turn_kernel,
        out_shape=pltpu.HBM((Y, 2, part, 2 * voc), BF16),
        in_specs=[pl.BlockSpec(memory_space=pltpu.SMEM), hbm, hbm],
        out_specs=hbm,
        scratch_shapes=[
            pltpu.VMEM((2 * Y, 2, voc, wide), BF16),
            pltpu.VMEM((2, 2, wide, voc), BF16),
            pltpu.VMEM((2 * Y, part, 2 * voc), BF16),
            pltpu.SemaphoreType.DMA((2 * Y, 2)),
            pltpu.SemaphoreType.DMA((2 * Y,)),
        ],
        compiler_params=pltpu.CompilerParams(vmem_limit_bytes=VMEM_LIMIT),
        cost_estimate=pl.CostEstimate(flops=0, bytes_accessed=12 * Y * voc * wide, transcendentals=0),
    )(meta, *in_hbm([own, other]))


FIRST_BLOCKS = ((0, 0), (1, 0), (2, 0), (3, 0), (2, 1))
REST_BLOCKS = ((0, 0), (1, 0), (2, 0), (3, 0), (0, 1), (1, 1), (3, 1))


def fetch_blocks(wt_ref, blocks, slots, sems):
    return [
        pltpu.make_async_copy(wt_ref.at[step, side], slots.at[i], sems.at[i]) for i, (step, side) in enumerate(blocks)
    ]


def product(slots, first, last, dls):
    blocks = slots[first:last].reshape((last - first) * slots.shape[1], slots.shape[2])
    return jnp.dot(blocks, dls, preferred_element_type=F32)


def first_kernel(base_ref, wt_ref, grown_ref, grown_other_ref, tgt_ref, vectors_ref, *refs):
    dls_ref, a_ref, b_ref, slots, sems = refs
    part, rows = a_ref.shape[1:]
    copies = fetch_blocks(wt_ref, FIRST_BLOCKS, slots, sems)
    start_all(copies)
    chunk = 64
    voc = grown_ref.shape[0]
    for i, source_ref in enumerate((grown_ref, grown_other_ref)):
        for low in range(0, voc, chunk):
            columns = base_ref[i] + low + lax.broadcasted_iota(jnp.int32, (chunk, dls_ref.shape[1]), 0)
            value = source_ref[low : low + chunk] * vectors_ref[0:1]
            value = jnp.where(columns == tgt_ref[...], vectors_ref[1:2], value)
            dls_ref[i * voc + low : i * voc + low + chunk] = value.astype(BF16)
    wait_all(copies)
    a = product(slots, 0, Y, dls_ref[:, 2 * rows : 3 * rows]).astype(BF16)
    for step in range(Y):
        a_ref[step] = a[step * part : (step + 1) * part]
    b_ref[...] = product(slots, Y, Y + 1, dls_ref[...]).astype(BF16)


def first_call(base, wt, grown, grown_other, tgt, vectors):
    vmem = pl.BlockSpec(memory_space=pltpu.VMEM)
    hbm = pl.BlockSpec(memory_space=pltpu.HBM)
    voc, all_rows = grown.shape
    part = wt.shape[2]
    dls = jax.ShapeDtypeStruct((2 * voc, all_rows), BF16)
    a_far = jax.ShapeDtypeStruct((Y, part, all_rows // X), BF16)
    b_far = jax.ShapeDtypeStruct((part, all_rows), BF16)
    count = len(FIRST_BLOCKS)
    return pl.pallas_call(
        first_kernel,
        out_shape=(dls, a_far, b_far),
        in_specs=[pl.BlockSpec(memory_space=pltpu.SMEM), hbm] + [vmem] * 4,
        out_specs=(vmem,) * 3,
        scratch_shapes=[
            pltpu.VMEM((count, part, 2 * voc), BF16),
            pltpu.SemaphoreType.DMA((count,)),
        ],
        compiler_params=pltpu.CompilerParams(vmem_limit_bytes=VMEM_LIMIT),
        cost_estimate=pl.CostEstimate(
            flops=2 * wt.size * all_rows // 4, bytes_accessed=wt.size + 8 * grown.size, transcendentals=0
        ),
    )(base, *in_hbm([wt]), grown, grown_other, tgt, vectors)


def rest_kernel(wt_ref, dls_ref, *refs):
    a_outs, b_outs = refs[:3], refs[3:6]
    slots, sems = refs[6:]
    part, rows = a_outs[0].shape[1:]
    copies = fetch_blocks(wt_ref, REST_BLOCKS, slots, sems)
    start_all(copies[:Y])
    wait_all(copies[:Y])
    start_all(copies[Y:])
    a = product(slots, 0, Y, dls_ref[...])
    for step in range(Y):
        for out_ref, place in zip(a_outs, (0, 1, 3)):
            out_ref[step] = a[step * part : (step + 1) * part, place * rows : (place + 1) * rows]
    wait_all(copies[Y:])
    b = product(slots, Y, Y + 3, dls_ref[...])
    for i, out_ref in enumerate(b_outs):
        out_ref[...] = b[i * part : (i + 1) * part]


def rest_call(outs, wt, dls):
    vmem = pl.BlockSpec(memory_space=pltpu.VMEM)
    part, wide = wt.shape[2:]
    count = len(REST_BLOCKS)
    return pl.pallas_call(
        rest_kernel,
        out_shape=tuple(outs),
        in_specs=[pl.BlockSpec(memory_space=pltpu.HBM), vmem],
        out_specs=tuple([vmem] * len(outs)),
        scratch_shapes=[pltpu.VMEM((count, part, wide), BF16), pltpu.SemaphoreType.DMA((count,))],
        compiler_params=pltpu.CompilerParams(vmem_limit_bytes=VMEM_LIMIT),
        cost_estimate=pl.CostEstimate(
            flops=2 * count * part * wide * dls.shape[1], bytes_accessed=2 * count * part * wide, transcendentals=0
        ),
    )(*in_hbm([wt]), dls)


def weight_kernel(places_ref, dl_ref, here_ref, there_ref, *refs):
    out_ref, both = refs[-2:]
    half = here_ref.shape[1]
    core = places_ref[Y]
    both[pl.ds(pl.multiple_of(core * half, 64), half)] = here_ref[0]
    both[pl.ds(pl.multiple_of((1 - core) * half, 64), half)] = there_ref[0]
    over_last = (((1,), (1,)), ((), ()))
    out_ref[...] = lax.dot_general(dl_ref[...], both[...], over_last, preferred_element_type=F32).astype(BF16)


def weight_of(places, dls, here, there, first, count, into=()):
    voc, all_rows = dls.shape[0] // 2, dls.shape[1]
    half = here.shape[1]
    one = pl.BlockSpec((1, half, all_rows), lambda i, places: (i + first, 0, 0))
    return pl.pallas_call(
        weight_kernel,
        out_shape=jax.ShapeDtypeStruct((voc, Y * 2 * half), BF16),
        grid_spec=pltpu.PrefetchScalarGridSpec(
            num_scalar_prefetch=1,
            grid=(count,),
            in_specs=[pl.BlockSpec((voc, all_rows), lambda i, places: (0, 0)), one, one] + [pl.BlockSpec(memory_space=pl.ANY)] * len(into),
            out_specs=pl.BlockSpec((voc, 2 * half), lambda i, places: (0, places[i + first])),
            scratch_shapes=[pltpu.VMEM((2 * half, all_rows), BF16)],
        ),
        input_output_aliases={4: 0} if into else {},
        compiler_params=pltpu.CompilerParams(vmem_limit_bytes=VMEM_LIMIT),
        cost_estimate=pl.CostEstimate(
            flops=4 * count * voc * half * all_rows, bytes_accessed=8 * count * half * all_rows, transcendentals=0
        ),
    )(places, dls, *in_hbm([here, there]), *into)


def per_device(hidden, weight, targets):
    rows, feats = hidden.shape
    voc = weight.shape[0]
    block = Z * C * feats
    half = block // 2
    part = half // 2
    pad = -half % 128
    wide = half + pad
    x, y, z, c = (lax.axis_index(name) for name in ("x", "y", "z", "c"))

    partner = flip(weight, "c", C, 1)
    along = spread(hidden.T, "z", Z)
    places = jnp.stack([y ^ step for step in range(Y)])
    lows = [c * half, c * half + part]
    windows = [places * block + low // 128 * 128 for low in lows]
    meta = jnp.concatenate(windows + [jnp.stack([low % 128 for low in lows])])
    wt = turned_weights(meta, weight, partner, part, -(-part // 128) * 128)
    along, wt = at_once(along, wt)
    along = along.reshape(2, Z // 2, feats, rows)
    keep = lax.dynamic_index_in_dim(along, c, 0, keepdims=False)
    give = lax.dynamic_index_in_dim(along, 1 - c, 0, keepdims=False)
    got = flip(give, "c", C, 1)
    along = jnp.stack([jnp.where(c == 0, keep, got), jnp.where(c == 0, got, keep)], 1).reshape(half, rows)
    a, b = along[:part], jnp.concatenate([along[part:], digits(targets)])
    a, b = at_once(a, b)
    a1, b1 = at_once(flip(a, "y", Y, 1), flip(b, "x", X, 1))
    a01, b01 = jnp.stack([a, a1]), jnp.stack([b, b1])
    a32, b32 = at_once(flip(a01, "y", Y, 3), flip(b01, "x", X, 3))
    a2 = jnp.stack([a01[0], a01[1], a32[1], a32[0]])
    b2 = jnp.stack([b01[0], b01[1], b32[1], b32[0]])
    tgt = undigits(b2[:, part:]).reshape(X * rows)
    a2, b2 = at_once(a2, b2[:, :part])
    ax1, by1, ax3, by3, ax2, by2 = at_once(
        *[flip(array, axis, 4, step) for step in (1, 3, 2) for array, axis in ((a2, "x"), (b2, "y"))]
    )
    meta = jnp.append(places * block + c * (half - pad), c * pad)

    mine, theirs, ht = logits_of(
        meta, weight, partner, [a2, ax1, ax2, ax3], [b2, by1, by2, by3], wide
    )
    theirs = flip(theirs, "c", C, 1)
    capped = CAP * jnp.tanh((mine + theirs) / CAP)
    offset = (((x * Y + y) * Z + z) * C + c) * voc
    columns = offset + jnp.arange(voc, dtype=jnp.int32)
    hit = columns[:, None] == tgt[None, :]
    stats = jnp.stack([jnp.sum(jnp.exp(capped - CAP), 0), jnp.sum(jnp.where(hit, capped, 0.0), 0)])
    stats, ht, mine, theirs = at_once(stats, ht, mine, theirs)
    other = flip(ht, "c", C, 1)
    capped = CAP * jnp.tanh((mine + theirs) / CAP)
    grown = jnp.exp(capped - CAP) * (1.0 - (capped / CAP) ** 2)
    stats = spread(stats.reshape(2, X, rows), ("z", "c"), Z * C).sum(0)
    stats = reordered(stats, x, 1)
    stats, grown, other = at_once(stats, grown, other)
    grown_other = flip(grown, "c", C, 1)
    stats = spread(stats, ("x", "y"), X * Y).sum(0)
    stats = reordered(stats, x, 1)
    stats, grown_other = at_once(stats, grown_other)
    lse = CAP + jnp.log(stats[0])
    loss = lse[0] - stats[1, 0]
    at_target = (jnp.exp(stats[1] - lse) - 1.0) * (1.0 - (stats[1] / CAP) ** 2)
    vectors = jnp.stack([(1.0 / stats[0]).reshape(-1), at_target.reshape(-1)])
    base = jnp.stack([offset, offset + (1 - 2 * c) * voc])

    dls, a_far, b_far = first_call(base, wt, grown, grown_other, tgt[None], vectors)
    a_far, b_far = at_once(flip(a_far, "x", X, 1), flip(b_far, "y", Y, 1))
    a_kind = jax.ShapeDtypeStruct((Y, part, rows), F32)
    b_kind = jax.ShapeDtypeStruct((part, X * rows), F32)
    a0, a1, a3, b0, b1, b3 = rest_call([a_kind] * 3 + [b_kind] * 3, wt, dls)
    a1, a3 = a1.astype(BF16), (a3 + a_far.astype(F32)).astype(BF16)
    b1, b3 = b1.astype(BF16), (b3 + b_far.astype(F32)).astype(BF16)
    begun = weight_of(jnp.append(places, c), dls, ht, other, 0, 1)
    a1, b1, a3, b3, begun = at_once(a1, b1, a3, b3, begun)
    a1, b1, a3, b3 = at_once(flip(a1, "x", X, 1), flip(b1, "y", Y, 1), flip(a3, "x", X, 3), flip(b3, "y", Y, 3))
    a_own = a0 + a1.astype(F32) + a3.astype(F32)
    b_own = b0 + b1.astype(F32) + b3.astype(F32)
    a_out, b_out = at_once(a_own[1:3].astype(BF16), b_own[:, rows : 3 * rows].astype(BF16))
    a_in, b_in = at_once(flip(a_out, "y", Y, 1), flip(b_out, "x", X, 1))
    a_out = (a_own[3] + a_in[1].astype(F32)).astype(BF16)
    b_out = (b_own[:, 3 * rows :] + b_in[:, rows:].astype(F32)).astype(BF16)
    a_out, b_out = at_once(a_out, b_out)
    a_out, b_out = at_once(flip(a_out, "y", Y, 3), flip(b_out, "x", X, 3))
    a_sum = a_own[0] + a_in[0].astype(F32) + a_out.astype(F32)
    b_sum = b_own[:, :rows] + b_in[:, :rows].astype(F32) + b_out.astype(F32)
    total = jnp.concatenate([a_sum, b_sum]).reshape(Z // 2, C, feats, rows)
    mine = lax.dynamic_index_in_dim(total, c, 1, keepdims=False)
    theirs = flip(lax.dynamic_index_in_dim(total, 1 - c, 1, keepdims=False), "c", C, 1)
    by_z = jnp.concatenate([jnp.where(c == 0, mine, theirs), jnp.where(c == 0, theirs, mine)])
    by_z, dls, begun = at_once(by_z, dls, begun)
    grad_weight = weight_of(jnp.append(places, c), dls, ht, other, 1, Y - 1, (begun,))
    grad_hidden = lax.all_to_all(by_z, "z", 0, 0, tiled=True).sum(0).astype(BF16).T
    return loss, grad_hidden, grad_weight


def solution(mesh):
    chips = Mesh(mesh.devices.reshape(X, Y, Z, C), ("x", "y", "z", "c"))
    in_specs = (P("x", ("y", "z", "c")), P(("x", "y", "z", "c"), None), P("x"))
    out_specs = (P("x"), P("x", ("y", "z", "c")), P(("x", "y", "z", "c"), None))
    return jax.shard_map(per_device, mesh=chips, in_specs=in_specs, out_specs=out_specs, check_vma=False)
```
